32 devices in a mesh: radius: 2 (over core), polar: 4 (over y, x), group: 4 (over z).
Axes of the slice: x: 2, y: 2, z: 4, core: 2. Of those that a mesh axis runs over, the one named last changes fastest.
Arguments:
- density: float32 [96, 1024], P('radius', 'polar'), may hold values from 0.3 to 3
- opacity: bfloat16 [64, 96, 1024], P('group', 'radius', 'polar'), may hold values from 0.049804688 to 5
- radiation_old: float32 [64, 96, 1024], P('group', 'radius', 'polar'), may hold values from 0.5 to 2
- material_old: float32 [96, 1024], P('radius', 'polar'), may hold values from 0.5 to 2
- weights: float32 [64], P('group'), may hold values from 0.5 to 2
- stellar_flux: float32 [96], P('radius'), may hold values from 10 to 100
Outputs:
- energy: float32 [64, 96, 1024], P('group', 'radius', 'polar')
- material_now: float32 [96, 1024], P('radius', 'polar')
- column: float32 [96, 1024], P('radius', 'polar')
The draws below stay inside these ranges and needn't reach their ends.
All inputs are finite; a program needn't handle non-finite values.
Results may differ from the reference program's by a relative error of at most 0.0003.
Values sent between devices are 32-bit elements; how exact they have to be, the bound alone decides.
A program may use at most 64 MiB of HBM per device.

```python
import math
import jax
import jax.numpy as jnp
from jax import lax

G = 64
ITERS = 3
SWEEPS = 2
NR = 96
NT = 1024


def block_levels(stream_key, shape, cuts, least, top_value):
    factor_of, own = 1.0, jax.random.fold_in(stream_key, 6)
    for position, blocks in cuts:
        draws = jnp.exp(jax.random.uniform(jax.random.fold_in(own, position), (blocks,), jnp.float32, least / len(cuts), top_value / len(cuts)))
        factor_of = factor_of * jnp.repeat(draws, shape[position] // blocks).reshape([-1 if axis == position else 1 for axis in range(len(shape))])
    return factor_of


def setup_inputs(seed: int = 0) -> dict:
    key_of = jax.random.split(jax.random.key(seed), 7)
    density = jnp.clip(jnp.exp(math.log(3.0) - 2.3025851 * jax.random.uniform(key_of[0], (NR, NT), jnp.float32) ** block_levels(key_of[0], (NR, NT), ((0, 2), (1, 4)), -0.2, 0.2)), 0.3, 3.0)
    opacity = jnp.clip(jnp.exp(math.log(5.0) - 4.609084 * jax.random.uniform(key_of[1], (G, NR, NT), jnp.float32) ** block_levels(key_of[1], (G, NR, NT), ((0, 4), (1, 2), (2, 4)), -0.2, 0.2)), 0.049804688, 5.0).astype(jnp.bfloat16)
    radiation_old = jnp.clip(0.5 + 1.5 * jax.random.uniform(key_of[2], (G, NR, NT), jnp.float32) ** block_levels(key_of[2], (G, NR, NT), ((0, 4), (1, 2), (2, 4)), -0.2, 0.2), 0.5, 2.0)
    material_old = jnp.clip(0.5 + 1.5 * jax.random.uniform(key_of[3], (NR, NT), jnp.float32) ** block_levels(key_of[3], (NR, NT), ((0, 2), (1, 4)), -0.2, 0.2), 0.5, 2.0)
    weights = jnp.clip(jnp.exp(math.log(2.0) - 1.3862944 * jax.random.uniform(key_of[4], (G,), jnp.float32) ** block_levels(key_of[4], (G,), ((0, 4),), -0.2, 0.2)), 0.5, 2.0)
    stellar_flux = jnp.clip(jnp.exp(math.log(100.0) - 2.3025851 * jax.random.uniform(key_of[5], (NR,), jnp.float32) ** block_levels(key_of[5], (NR,), ((0, 2),), -0.2, 0.2)), 10.0, 100.0)
    return dict(density=density, opacity=opacity, radiation_old=radiation_old, material_old=material_old, weights=weights, stellar_flux=stellar_flux)


def harmonic(lower_value, upper_value):
    return 2.0 * lower_value * upper_value / (lower_value + upper_value)

def limited_diffusion(old_field, absorb):
    padded = jnp.pad(old_field, 1)
    radial_slope = 0.5 * (padded[2:, 1:-1] - padded[:-2, 1:-1])
    polar_slope = 0.5 * (padded[1:-1, 2:] - padded[1:-1, :-2])
    ratio_value = jnp.sqrt(radial_slope * radial_slope + polar_slope * polar_slope) / (absorb * old_field)
    limiter = (2.0 + ratio_value) / (6.0 + 3.0 * ratio_value + ratio_value * ratio_value)
    return limiter / absorb

def face_terms(diffusion):
    padded = jnp.pad(diffusion, 1)
    return (harmonic(diffusion, padded[2:, 1:-1]), harmonic(padded[:-2, 1:-1], diffusion), harmonic(diffusion, padded[1:-1, 2:]), harmonic(padded[1:-1, :-2], diffusion))

def apply_operator(field, absorb, face_coeffs):
    padded = jnp.pad(field, 1)
    return (1.0 + absorb) * field + face_coeffs[0] * (field - padded[2:, 1:-1]) + face_coeffs[1] * (field - padded[:-2, 1:-1]) + face_coeffs[2] * (field - padded[1:-1, 2:]) + face_coeffs[3] * (field - padded[1:-1, :-2])

def solve_group(energy, residual, absorb, face_coeffs):
    norm_now = jnp.sum(residual * residual)
    direction = residual
    for sweep_index in range(SWEEPS):
        applied = apply_operator(direction, absorb, face_coeffs)
        step_size = norm_now / jnp.sum(direction * applied)
        energy = energy + step_size * direction
        residual = residual - step_size * applied
        if sweep_index + 1 < SWEEPS:
            norm_next = jnp.sum(residual * residual)
            direction = residual + norm_next / norm_now * direction
            norm_now = norm_next
    return (energy, residual)

def reference(density, opacity, radiation_old, material_old, weights, stellar_flux):
    column = 2.0 / NT * jnp.cumsum(density, axis=1)
    heating = stellar_flux[:, None] * density * jnp.exp(-column)

    def emission_term(running, group_item):
        opacity_row, weight = group_item
        return (running + opacity_row.astype(jnp.float32) * density * weight, None)
    emission, _ = lax.scan(emission_term, jnp.zeros_like(density), (opacity, weights))
    capacity = 16.0 * density + emission
    energy = radiation_old
    residual = radiation_old
    material_now = material_old
    material_prev = material_old
    for round_index in range(ITERS):

        def group_step(running, group_item):
            opacity_row, old_field, weight, energy_row, residual_row = group_item
            absorb = opacity_row.astype(jnp.float32) * density
            face_coeffs = face_terms(limited_diffusion(old_field, absorb))
            if round_index == 0:
                residual_row = absorb * weight * material_old + old_field - apply_operator(old_field, absorb, face_coeffs)
            else:
                residual_row = residual_row + absorb * weight * (material_now - material_prev)
            energy_row, residual_row = solve_group(energy_row, residual_row, absorb, face_coeffs)
            return (running + absorb * energy_row, (energy_row, residual_row))
        absorbed, (energy, residual) = lax.scan(group_step, jnp.zeros_like(density), (opacity, radiation_old, weights, energy, residual))
        material_next = (16.0 * density * material_old + heating + absorbed) / capacity
        material_prev = material_now
        material_now = material_next
    return (energy, material_now, column)
```

```python
import functools

import jax
import jax.numpy as jnp
from jax import lax
from jax.experimental import pallas as pl
from jax.experimental.pallas import tpu as pltpu
from jax.sharding import PartitionSpec as P

ITERS = 3
LANES = 128
SUB = 8
MESH = pl.DeviceIdType.MESH
HI = lax.Precision.HIGHEST


def harm(a, b):
    total = a + b
    return 2.0 * a * b / jnp.where(total > 0.0, total, 1.0)


def kernel(
    nr, npol, nz,
    dens, opac, rad, mat0, wts, flux,
    e_out, m_out, col_out,
    e_x, a_x, d_x, r_x, dg_x, fu_x, fd_x, fl_x, fr_x, ar, aar,
    o_ea, hl_ea, hr_ea, o_d, hl_d, hr_d, o_r, hl_r, hr_r,
    halo_x, halo_ar, gsum, gram, cres, cimg,
    rows_src, rows_buf, absb, emis, rsbuf, mnext, fixed, capac, dmat,
    slab_s, slab_v, pol_s, pol_v, diag_s, diag_v,
    gram_s, gram_v, rs_s, rs_v, ag_s, ag_v, row_s, row_v,
):
    ng, nrow, ncol = rad.shape
    nt = ncol // LANES
    next_ = nrow + 2 * SUB
    own = slice(SUB, SUB + nrow)
    tiles = (nrow // SUB) * nt
    tp = tiles // nz
    plane = nr * npol

    ir = lax.axis_index("radius")
    ip = lax.axis_index("polar")
    iz = lax.axis_index("group")
    me = ir * npol + ip

    def lane_of(n):
        return lax.broadcasted_iota(jnp.int32, (n, LANES), 1)

    lane_own, lane_ext = lane_of(nrow), lane_of(next_)

    def zeros_at(ref, *idx):
        ref[idx] = jnp.zeros(ref.at[idx].shape, ref.dtype)

    for ref in (e_x, a_x, d_x, r_x):
        zeros_at(ref, slice(None), slice(0, SUB), slice(None))
        zeros_at(ref, slice(None), slice(SUB + nrow, next_), slice(None))
    for ref in (hl_ea, hr_ea, hl_d, hr_d, hl_r, hr_r, rows_buf):
        ref[...] = jnp.zeros(ref.shape, ref.dtype)

    barrier = pltpu.get_barrier_semaphore()

    def plane_id(k):
        other = lax.rem(me + k, plane)
        return other, {"radius": other // npol, "polar": lax.rem(other, npol)}

    @pl.loop(1, plane)
    def _(k):
        _, where = plane_id(k)
        pl.semaphore_signal(barrier, inc=1, device_id=where, device_id_type=MESH)

    for k in range(1, nz):
        pl.semaphore_signal(
            barrier, inc=1, device_id={"group": lax.rem(iz + k, nz)}, device_id_type=MESH
        )

    def remote(src, dst, ssem, rsem, where):
        return pltpu.make_async_remote_copy(
            src_ref=src, dst_ref=dst, send_sem=ssem, recv_sem=rsem,
            device_id=where, device_id_type=MESH,
        )

    def near(dr, dp):
        return {"radius": lax.rem(ir + dr + nr, nr), "polar": lax.rem(ip + dp + npol, npol)}

    def inside(dr, dp):
        r, p = ir + dr, ip + dp
        return (r >= 0) & (r < nr) & (p >= 0) & (p < npol)

    def slab_copies(src_ref, lo, hi, dst_ref, f):
        out = []
        for i, dr in enumerate((-1, 1)):
            src = src_ref.at[:, pl.ds(lo if dr < 0 else hi, SUB), :]
            dst = dst_ref.at[:, pl.ds(SUB + nrow if dr < 0 else 0, SUB), :]
            out.append((dr, 0, remote(src, dst, slab_s.at[f, i], slab_v.at[f, i], near(dr, 0))))
        return out

    def pol_copies(o, hl, hr, f):
        out = []
        for i, dp in enumerate((-1, 1)):
            dst = (hr if dp < 0 else hl).at[:, pl.ds(SUB, nrow), :]
            out.append((0, dp, remote(o, dst, pol_s.at[f, i], pol_v.at[f, i], near(0, dp))))
        return out

    def diag_copies(o, hl, hr, f):
        out = []
        for i, (dr, dp) in enumerate(((-1, -1), (-1, 1), (1, -1), (1, 1))):
            src = o.at[:, pl.ds(0 if dr < 0 else nrow - SUB, SUB), :]
            dst = (hr if dp < 0 else hl).at[:, pl.ds(SUB + nrow if dr < 0 else 0, SUB), :]
            out.append((dr, dp, remote(src, dst, diag_s.at[f, i], diag_v.at[f, i], near(dr, dp))))
        return out

    def start(copies):
        for dr, dp, c in copies:
            @pl.when(inside(dr, dp))
            def _():
                c.start()

    def finish(copies):
        for dr, dp, c in copies:
            @pl.when(inside(-dr, -dp))
            def _():
                c.wait_recv()
        for dr, dp, c in copies:
            @pl.when(inside(dr, dp))
            def _():
                c.wait_send()

    def load(ref, g, rows):
        return [ref[g, rows, k * LANES:(k + 1) * LANES] for k in range(nt)]

    def pack(tiles_in, g, into):
        left = pltpu.roll(tiles_in[0], 2 * g, 1)
        right = pltpu.roll(tiles_in[-1], lax.rem(2 * g + LANES // 2 + 2, LANES), 1)
        half = lane_own // 2
        into = jnp.where(half == g, left, into)
        return jnp.where(half == g + LANES // 4, right, into)

    def left_of(v, halo, g):
        n = v[0].shape[0]
        edge = lane_of(n) == 0
        turned = [pltpu.roll(t, 1, 1) for t in v]
        before = [pltpu.roll(halo, LANES // 2 - 1 - 2 * g, 1)] + turned[:-1]
        return [jnp.where(edge, b, t) for b, t in zip(before, turned)]

    def right_of(v, halo, g):
        n = v[0].shape[0]
        edge = lane_of(n) == LANES - 1
        turned = [pltpu.roll(t, LANES - 1, 1) for t in v]
        after = turned[1:] + [pltpu.roll(halo, LANES - 1 - 2 * g, 1)]
        return [jnp.where(edge, b, t) for b, t in zip(after, turned)]

    def above(t):
        return pltpu.roll(t, 1, 0)

    def below(t):
        return pltpu.roll(t, t.shape[0] - 1, 0)

    def both(hl, hr, k):
        return jnp.where(lane_ext < LANES // 2, hr[k], hl[k])

    def outer_of(x):
        n = x.shape[0]
        return jnp.where(lane_of(n) < LANES // 2, pltpu.roll(x, LANES - 1, 1), pltpu.roll(x, 1, 1))

    def inner_of(o):
        return jnp.where(
            lane_own < LANES // 2,
            pltpu.roll(o, LANES // 2 - 1, 1),
            pltpu.roll(o, LANES // 2 + 1, 1),
        )

    zero_pack = jnp.zeros((nrow, LANES), jnp.float32)
    zero_tiles = tuple(jnp.zeros((nrow, LANES), jnp.float32) for _ in range(nt))

    def put_tiles(ref, parts):
        for k, part in enumerate(parts):
            for i in range(nrow // SUB):
                ref[k * (nrow // SUB) + i] = part[i * SUB:(i + 1) * SUB]

    def get_tiles(ref):
        per = nrow // SUB
        return [
            jnp.concatenate([ref[k * per + i] for i in range(per)], axis=0) for k in range(nt)
        ]

    def scatter_copies(src, slot):
        out = []
        for k in range(1, nz):
            to = lax.rem(iz + k, nz)
            out.append(remote(
                src.at[pl.ds(to * tp, tp)], rsbuf.at[slot, iz],
                rs_s.at[slot, k], rs_v.at[slot, k], {"group": to},
            ))
        return out

    def gathered_sum(src, slot, copies):
        rsbuf[slot, iz] = src[pl.ds(iz * tp, tp)]
        for c in copies:
            c.wait_recv()
        total = rsbuf[slot, 0]
        for k in range(1, nz):
            total = total + rsbuf[slot, k]
        return total

    dens_t = [dens[:, k * LANES:(k + 1) * LANES] for k in range(nt)]

    def first(g, carry):
        oe, oa, em = carry
        a = [
            opac[g, :, k * LANES:(k + 1) * LANES].astype(jnp.float32) * dens_t[k]
            for k in range(nt)
        ]
        for k in range(nt):
            a_x[g, own, k * LANES:(k + 1) * LANES] = a[k]
            e_x[g, own, k * LANES:(k + 1) * LANES] = rad[g, :, k * LANES:(k + 1) * LANES]
        em = tuple(em[k] + a[k] * wts[g] for k in range(nt))
        return pack(load(rad, g, slice(None)), g, oe), pack(a, g, oa), em

    oe, oa, em = lax.fori_loop(0, ng, first, (zero_pack, zero_pack, zero_tiles))
    o_ea[0] = oe
    o_ea[1] = oa
    put_tiles(emis, em)
    rows = sum(jnp.sum(t, axis=1, keepdims=True) for t in dens_t)
    rows_src[...] = jnp.broadcast_to(rows, (nrow, LANES))

    pl.semaphore_wait(barrier, plane - 1 + nz - 1)

    ea = (
        slab_copies(e_x, SUB, nrow, e_x, 0)
        + slab_copies(a_x, SUB, nrow, a_x, 1)
        + pol_copies(o_ea, hl_ea, hr_ea, 0)
    )
    start(ea)
    emit = scatter_copies(emis, ITERS)
    for c in emit:
        c.start()
    prefix = []
    for k in range(1, npol):
        to = lax.rem(ip + k, npol)
        prefix.append((
            ip + k < npol, ip - k >= 0,
            remote(rows_src, rows_buf.at[ip], row_s.at[k], row_v.at[k], {"polar": to}),
        ))
    for sends, _, c in prefix:
        @pl.when(sends)
        def _():
            c.start()

    tri = (
        lax.broadcasted_iota(jnp.int32, (ncol, ncol), 0)
        <= lax.broadcasted_iota(jnp.int32, (ncol, ncol), 1)
    ).astype(jnp.float32)
    within = jnp.dot(dens[...], tri, precision=HI, preferred_element_type=jnp.float32)
    col_out[...] = within
    finish(ea)

    x_e = both(hl_ea, hr_ea, 0)
    x_a = both(hl_ea, hr_ea, 1)
    halo_x[...] = x_e

    def second(g, od):
        v = load(e_x, g, slice(None))
        a = load(a_x, g, own)
        x = halo_x[own]
        v_own = [t[own] for t in v]
        lft, rgt = left_of(v_own, x, g), right_of(v_own, x, g)
        d = []
        for k in range(nt):
            rs = 0.5 * (below(v[k])[own] - above(v[k])[own])
            ps = 0.5 * (rgt[k] - lft[k])
            s = jnp.sqrt(rs * rs + ps * ps)
            q = a[k] * v_own[k]
            d.append(v_own[k] * (2.0 * q + s) / (6.0 * q * q + 3.0 * q * s + s * s))
            d_x[g, own, k * LANES:(k + 1) * LANES] = d[k]
        return pack(d, g, od)

    o_d[0] = lax.fori_loop(0, ng, second, zero_pack)
    dd = slab_copies(d_x, SUB, nrow, d_x, 2) + pol_copies(o_d, hl_d, hr_d, 1) + diag_copies(
        o_d, hl_d, hr_d, 0
    )
    start(dd)

    for _, comes, c in prefix:
        @pl.when(comes)
        def _():
            c.wait_recv()
    carried = rows_buf[0]
    for k in range(1, npol):
        carried = carried + rows_buf[k]
    diag = (
        lax.broadcasted_iota(jnp.int32, (nrow, nrow), 0)
        == lax.broadcasted_iota(jnp.int32, (nrow, nrow), 1)
    )
    flux_col = jnp.sum(jnp.where(diag, flux[...], 0.0), axis=1, keepdims=True)
    fix = []
    for k in range(nt):
        sl = slice(k * LANES, (k + 1) * LANES)
        column = (2.0 / (ncol * npol)) * (carried + col_out[:, sl])
        col_out[:, sl] = column
        fix.append(
            16.0 * dens_t[k] * mat0[:, sl] + flux_col * dens_t[k] * jnp.exp(-column)
        )
    put_tiles(fixed, fix)
    put_tiles(capac, [16.0 * t for t in dens_t])
    emission = gathered_sum(emis, ITERS, emit)
    mine = pl.ds(iz * tp, tp)
    capac[mine] = capac[mine] + emission
    finish(dd)

    x_d = both(hl_d, hr_d, 0)
    d_in, d_out = inner_of(o_d[0]), outer_of(x_d)[own]
    x_mid = x_d[own]
    p_in, p_out = harm(x_mid, d_in), harm(x_mid, d_out)
    p_up, p_dn = harm(x_mid, above(x_d)[own]), harm(x_mid, below(x_d)[own])
    p_dg = 1.0 + x_a[own] + p_in + p_out + p_up + p_dn
    halo_ar[0] = p_in
    halo_ar[1] = p_out
    halo_ar[2] = p_up
    halo_ar[3] = p_dn
    halo_ar[4] = p_dg
    gsum[...] = jnp.zeros(gsum.shape, jnp.float32)
    mat_t = [mat0[:, k * LANES:(k + 1) * LANES] for k in range(nt)]
    d_halo = aar
    del d_halo
    hl_d[0] = x_d

    def third(g, o):
        d = load(d_x, g, slice(None))
        a = load(a_x, g, slice(None))
        v = load(e_x, g, slice(None))
        x = hl_d[0]
        xe = halo_x[own]
        dl, dr = left_of(d, x, g), right_of(d, x, g)
        v_own = [t[own] for t in v]
        vl, vr = left_of(v_own, xe, g), right_of(v_own, xe, g)
        res = []
        for k in range(nt):
            sl = slice(k * LANES, (k + 1) * LANES)
            fl, fr, fu = harm(d[k], dl[k]), harm(d[k], dr[k]), harm(d[k], above(d[k]))
            fd = below(fu)
            dg = 1.0 + a[k] + fl + fr + fu + fd
            fl_x[g, :, sl] = fl
            fr_x[g, :, sl] = fr
            fu_x[g, :, sl] = fu
            fd_x[g, :, sl] = fd
            dg_x[g, :, sl] = dg
            c = v_own[k]
            ao = a[k][own]
            image = (
                (1.0 + ao) * c
                + fu[own] * (c - above(v[k])[own])
                + fd[own] * (c - below(v[k])[own])
                + fl[own] * (c - vl[k])
                + fr[own] * (c - vr[k])
            )
            r = ao * wts[g] * mat_t[k] + c - image
            res.append(r)
            r_x[g, own, sl] = r
            e_out[g, :, sl] = c
        return pack(res, g, o)

    o_r[0] = lax.fori_loop(0, ng, third, zero_pack)
    m_out[...] = mat0[...]

    ones = jnp.ones((SUB, LANES), jnp.float32)
    quants = 4 * ng
    pick = (
        lax.broadcasted_iota(jnp.int32, (quants, LANES), 0)
        == lax.broadcasted_iota(jnp.int32, (quants, LANES), 1)
    )

    @pl.loop(0, ITERS)
    def _(it):
        rr = slab_copies(r_x, SUB, nrow, r_x, 3) + pol_copies(o_r, hl_r, hr_r, 2) + diag_copies(
            o_r, hl_r, hr_r, 1
        )
        start(rr)
        finish(rr)
        x_r = both(hl_r, hr_r, 0)
        halo_x[...] = x_r
        x_own = x_r[own]
        halo_ar[5] = (
            halo_ar[4] * x_own
            - halo_ar[0] * inner_of(o_r[0])
            - halo_ar[1] * outer_of(x_r)[own]
            - halo_ar[2] * above(x_r)[own]
            - halo_ar[3] * below(x_r)[own]
        )

        @pl.loop(0, ng)
        def _(g):
            v = load(r_x, g, slice(None))
            x = halo_x[...]
            vl, vr = left_of(v, x, g), right_of(v, x, g)
            w = []
            for k in range(nt):
                sl = slice(k * LANES, (k + 1) * LANES)
                w.append(
                    dg_x[g, :, sl] * v[k]
                    - fu_x[g, :, sl] * above(v[k])
                    - fd_x[g, :, sl] * below(v[k])
                    - fl_x[g, :, sl] * vl[k]
                    - fr_x[g, :, sl] * vr[k]
                )
            w_own = [t[own] for t in w]
            wx = halo_ar[5]
            wl, wr = left_of(w_own, wx, g), right_of(w_own, wx, g)
            sums = [0.0, 0.0, 0.0, 0.0]
            for k in range(nt):
                sl = slice(k * LANES, (k + 1) * LANES)
                c = w_own[k]
                t = (
                    dg_x[g, own, sl] * c
                    - fu_x[g, own, sl] * above(w[k])[own]
                    - fd_x[g, own, sl] * below(w[k])[own]
                    - fl_x[g, own, sl] * wl[k]
                    - fr_x[g, own, sl] * wr[k]
                )
                ar[g, :, sl] = c
                aar[g, :, sl] = t
                r = v[k][own]
                for i, (p, q) in enumerate(((r, r), (r, c), (c, c), (c, t))):
                    sums[i] = sums[i] + jnp.sum(p * q, axis=0, keepdims=True)
            for i in range(4):
                gsum[pl.ds(i * ng + g, 1), :] = sums[i]

        gram[it, me] = lax.dot_general(
            ones, gsum[...], (((1,), (1,)), ((), ())), precision=HI,
            preferred_element_type=jnp.float32,
        )

        def gram_copy(k):
            _, where = plane_id(k)
            return remote(
                gram.at[it, me], gram.at[it, me], gram_s.at[k], gram_v.at[it, k], where
            )

        @pl.loop(1, plane)
        def _(k):
            gram_copy(k).start()

        @pl.loop(1, plane)
        def _(k):
            c = gram_copy(k)
            c.wait_recv()
            c.wait_send()

        total = lax.fori_loop(
            0, plane, lambda k, s: s + gram[it, k], jnp.zeros((SUB, LANES), jnp.float32)
        )
        spread = jnp.sum(jnp.where(pick, total[0:1], 0.0), axis=1, keepdims=True)
        norm_first = spread[0:ng]
        first_curv = spread[ng:2 * ng]
        image_norm = spread[2 * ng:3 * ng]
        image_twice = spread[3 * ng:4 * ng]
        step_first = norm_first / first_curv
        norm_second = (
            norm_first - 2.0 * step_first * first_curv + step_first * step_first * image_norm
        )
        scaled = 1.0 + norm_second / norm_first
        second_curv = (
            scaled * scaled * first_curv
            - scaled * step_first * (2.0 * image_norm)
            + step_first * step_first * image_twice
        )
        step_second = norm_second / second_curv
        cres[...] = jnp.broadcast_to(step_first + step_second * scaled, (ng, LANES))
        cimg[...] = jnp.broadcast_to(step_second * step_first, (ng, LANES))

        def update(g, absorbed):
            cr = cres[pl.ds(g, 1), :]
            ci = cimg[pl.ds(g, 1), :]
            out = []
            for k in range(nt):
                sl = slice(k * LANES, (k + 1) * LANES)
                r, w = r_x[g, own, sl], ar[g, :, sl]
                e = e_out[g, :, sl] + cr * r - ci * w
                e_out[g, :, sl] = e
                r_x[g, own, sl] = r - cr * w + ci * aar[g, :, sl]
                out.append(absorbed[k] + a_x[g, own, sl] * e)
            return tuple(out)

        put_tiles(absb, lax.fori_loop(0, ng, update, zero_tiles))
        send = scatter_copies(absb, it)
        for c in send:
            c.start()
        mnext[it, mine] = (fixed[mine] + gathered_sum(absb, it, send)) / capac[mine]
        give = []
        for k in range(1, nz):
            give.append(remote(
                mnext.at[it, mine], mnext.at[it, mine],
                ag_s.at[it, k], ag_v.at[it, k], {"group": lax.rem(iz + k, nz)},
            ))
        for c in give:
            c.start()
        for c in give:
            c.wait_recv()
        for c in give + send:
            c.wait_send()
        news = get_tiles(mnext.at[it])
        for k in range(nt):
            sl = slice(k * LANES, (k + 1) * LANES)
            dmat[:, sl] = news[k] - m_out[:, sl]
            m_out[:, sl] = news[k]

        @pl.when(it + 1 < ITERS)
        def _():
            def feed(g, o):
                res = []
                for k in range(nt):
                    sl = slice(k * LANES, (k + 1) * LANES)
                    r = r_x[g, own, sl] + a_x[g, own, sl] * wts[g] * dmat[:, sl]
                    r_x[g, own, sl] = r
                    res.append(r)
                return pack(res, g, o)

            o_r[0] = lax.fori_loop(0, ng, feed, zero_pack)

    for c in emit:
        c.wait_send()
    for sends, _, c in prefix:
        @pl.when(sends)
        def _():
            c.wait_send()


def per_device(nr, npol, nz, density, opacity, radiation_old, material_old, weights, stellar_flux):
    ng, nrow, ncol = radiation_old.shape
    f32 = jnp.float32
    ext, inner = (ng, nrow + 2 * SUB, ncol), (ng, nrow, ncol)
    tiles = (nrow // SUB) * (ncol // LANES)
    plane = nr * npol
    vm = lambda *shape: pltpu.VMEM(shape, f32)
    packed, around = (nrow, LANES), (nrow + 2 * SUB, LANES)
    dma = lambda *shape: pltpu.SemaphoreType.DMA(shape)
    scratch = (
        [vm(*ext) for _ in range(9)]
        + [vm(*inner), vm(*inner)]
        + [vm(2, *packed), vm(2, *around), vm(2, *around)]
        + [vm(1, *packed), vm(1, *around), vm(1, *around)] * 2
        + [vm(*around), vm(6, *packed), vm(LANES, LANES), vm(ITERS, plane, SUB, LANES)]
        + [vm(ng, LANES), vm(ng, LANES)]
        + [vm(*packed), vm(npol, *packed), vm(tiles, SUB, LANES), vm(tiles, SUB, LANES)]
        + [vm(ITERS + 1, nz, tiles // nz, SUB, LANES), vm(ITERS, tiles, SUB, LANES)]
        + [vm(tiles, SUB, LANES), vm(tiles, SUB, LANES), vm(nrow, ncol)]
        + [dma(4, 2), dma(4, 2), dma(3, 2), dma(3, 2), dma(2, 4), dma(2, 4)]
        + [dma(plane), dma(ITERS, plane), dma(ITERS + 1, nz), dma(ITERS + 1, nz)]
        + [dma(ITERS, nz), dma(ITERS, nz), dma(npol), dma(npol)]
    )
    in_vmem = pl.BlockSpec(memory_space=pltpu.VMEM)
    return pl.pallas_call(
        functools.partial(kernel, nr, npol, nz),
        out_shape=[
            jax.ShapeDtypeStruct(inner, f32),
            jax.ShapeDtypeStruct((nrow, ncol), f32),
            jax.ShapeDtypeStruct((nrow, ncol), f32),
        ],
        in_specs=[in_vmem] * 4 + [pl.BlockSpec(memory_space=pltpu.SMEM), in_vmem],
        out_specs=[in_vmem] * 3,
        scratch_shapes=scratch,
        compiler_params=pltpu.CompilerParams(
            collective_id=0, has_side_effects=True, vmem_limit_bytes=48 * 1024 * 1024
        ),
    )(density, opacity, radiation_old, material_old, weights, stellar_flux.reshape(1, -1))


def solution(mesh):
    sizes = (mesh.shape["radius"], mesh.shape["polar"], mesh.shape["group"])
    return jax.shard_map(
        functools.partial(per_device, *sizes),
        mesh=mesh,
        in_specs=(
            P("radius", "polar"),
            P("group", "radius", "polar"),
            P("group", "radius", "polar"),
            P("radius", "polar"),
            P("group"),
            P("radius"),
        ),
        out_specs=(P("group", "radius", "polar"), P("radius", "polar"), P("radius", "polar")),
        check_vma=False,
    )
```

```python
import functools

import jax
import jax.numpy as jnp
from jax import lax
from jax.experimental import pallas as pl
from jax.experimental.pallas import tpu as pltpu
from jax.sharding import PartitionSpec as P

ITERS = 3
LANES = 128
SUB = 8
MESH = pl.DeviceIdType.MESH
HI = lax.Precision.HIGHEST


def harm(a, b):
    total = a + b
    return 2.0 * a * b / jnp.where(total > 0.0, total, 1.0)


def kernel(
    nr, npol, nz,
    dens, opac, rad, mat0, wts, flux,
    e_out, m_out, col_out,
    e_x, a_x, d_x, r_x, dg_x, fu_x, fd_x, fl_x, fr_x, ar, aar,
    o_ea, hl_ea, hr_ea, o_d, hl_d, hr_d, o_r, hl_r, hr_r,
    o_aw, halo_x, halo_ar, gsum, gram, cres, cimg,
    rows_src, rows_buf, absb, emis, rsbuf, mnext, fixed, capac, dmat,
    slab_s, slab_v, pol_s, pol_v, diag_s, diag_v,
    gram_s, gram_v, rs_s, rs_v, ag_s, ag_v, row_s, row_v,
):
    ng, nrow, ncol = rad.shape
    nt = ncol // LANES
    next_ = nrow + 2 * SUB
    own = slice(SUB, SUB + nrow)
    tiles = (nrow // SUB) * nt
    tp = tiles // nz
    plane = nr * npol

    ir = lax.axis_index("radius")
    ip = lax.axis_index("polar")
    iz = lax.axis_index("group")
    me = ir * npol + ip

    def lane_of(n):
        return lax.broadcasted_iota(jnp.int32, (n, LANES), 1)

    lane_own, lane_ext = lane_of(nrow), lane_of(next_)

    def zeros_at(ref, *idx):
        ref[idx] = jnp.zeros(ref.at[idx].shape, ref.dtype)

    for ref in (e_x, a_x, d_x, r_x):
        zeros_at(ref, slice(None), slice(0, SUB), slice(None))
        zeros_at(ref, slice(None), slice(SUB + nrow, next_), slice(None))
    for ref in (hl_ea, hr_ea, hl_d, hr_d, hl_r, hr_r, rows_buf):
        ref[...] = jnp.zeros(ref.shape, ref.dtype)

    barrier = pltpu.get_barrier_semaphore()

    def plane_id(k):
        other = lax.rem(me + k, plane)
        return other, {"radius": other // npol, "polar": lax.rem(other, npol)}

    @pl.loop(1, plane)
    def _(k):
        _, where = plane_id(k)
        pl.semaphore_signal(barrier, inc=1, device_id=where, device_id_type=MESH)

    for k in range(1, nz):
        pl.semaphore_signal(
            barrier, inc=1, device_id={"group": lax.rem(iz + k, nz)}, device_id_type=MESH
        )

    def remote(src, dst, ssem, rsem, where):
        return pltpu.make_async_remote_copy(
            src_ref=src, dst_ref=dst, send_sem=ssem, recv_sem=rsem,
            device_id=where, device_id_type=MESH,
        )

    def near(dr, dp):
        return {"radius": lax.rem(ir + dr + nr, nr), "polar": lax.rem(ip + dp + npol, npol)}

    def inside(dr, dp):
        r, p = ir + dr, ip + dp
        return (r >= 0) & (r < nr) & (p >= 0) & (p < npol)

    def slab_copies(src_ref, lo, hi, dst_ref, f):
        out = []
        for i, dr in enumerate((-1, 1)):
            src = src_ref.at[:, pl.ds(lo if dr < 0 else hi, SUB), :]
            dst = dst_ref.at[:, pl.ds(SUB + nrow if dr < 0 else 0, SUB), :]
            out.append((dr, 0, remote(src, dst, slab_s.at[f, i], slab_v.at[f, i], near(dr, 0))))
        return out

    def pol_copies(o, hl, hr, f):
        out = []
        for i, dp in enumerate((-1, 1)):
            dst = (hr if dp < 0 else hl).at[:, pl.ds(SUB, nrow), :]
            out.append((0, dp, remote(o, dst, pol_s.at[f, i], pol_v.at[f, i], near(0, dp))))
        return out

    def diag_copies(o, hl, hr, f):
        out = []
        for i, (dr, dp) in enumerate(((-1, -1), (-1, 1), (1, -1), (1, 1))):
            src = o.at[:, pl.ds(0 if dr < 0 else nrow - SUB, SUB), :]
            dst = (hr if dp < 0 else hl).at[:, pl.ds(SUB + nrow if dr < 0 else 0, SUB), :]
            out.append((dr, dp, remote(src, dst, diag_s.at[f, i], diag_v.at[f, i], near(dr, dp))))
        return out

    def start(copies):
        for dr, dp, c in copies:
            @pl.when(inside(dr, dp))
            def _():
                c.start()

    def finish(copies):
        for dr, dp, c in copies:
            @pl.when(inside(-dr, -dp))
            def _():
                c.wait_recv()
        for dr, dp, c in copies:
            @pl.when(inside(dr, dp))
            def _():
                c.wait_send()

    def load(ref, g, rows):
        return [ref[g, rows, k * LANES:(k + 1) * LANES] for k in range(nt)]

    def pack(tiles_in, g, into):
        left = pltpu.roll(tiles_in[0], 2 * g, 1)
        right = pltpu.roll(tiles_in[-1], lax.rem(2 * g + LANES // 2 + 2, LANES), 1)
        half = lane_own // 2
        into = jnp.where(half == g, left, into)
        return jnp.where(half == g + LANES // 4, right, into)

    def left_of(v, halo, g):
        n = v[0].shape[0]
        edge = lane_of(n) == 0
        turned = [pltpu.roll(t, 1, 1) for t in v]
        before = [pltpu.roll(halo, LANES // 2 - 1 - 2 * g, 1)] + turned[:-1]
        return [jnp.where(edge, b, t) for b, t in zip(before, turned)]

    def right_of(v, halo, g):
        n = v[0].shape[0]
        edge = lane_of(n) == LANES - 1
        turned = [pltpu.roll(t, LANES - 1, 1) for t in v]
        after = turned[1:] + [pltpu.roll(halo, LANES - 1 - 2 * g, 1)]
        return [jnp.where(edge, b, t) for b, t in zip(after, turned)]

    def above(t):
        return pltpu.roll(t, 1, 0)

    def below(t):
        return pltpu.roll(t, t.shape[0] - 1, 0)

    def both(hl, hr, k):
        return jnp.where(lane_ext < LANES // 2, hr[k], hl[k])

    def outer_of(x):
        n = x.shape[0]
        return jnp.where(lane_of(n) < LANES // 2, pltpu.roll(x, LANES - 1, 1), pltpu.roll(x, 1, 1))

    def inner_of(o):
        return jnp.where(
            lane_own < LANES // 2,
            pltpu.roll(o, LANES // 2 - 1, 1),
            pltpu.roll(o, LANES // 2 + 1, 1),
        )

    zero_pack = jnp.zeros((nrow, LANES), jnp.float32)
    zero_tiles = tuple(jnp.zeros((nrow, LANES), jnp.float32) for _ in range(nt))

    def put_tiles(ref, parts):
        for k, part in enumerate(parts):
            for i in range(nrow // SUB):
                ref[k * (nrow // SUB) + i] = part[i * SUB:(i + 1) * SUB]

    def get_tiles(ref):
        per = nrow // SUB
        return [
            jnp.concatenate([ref[k * per + i] for i in range(per)], axis=0) for k in range(nt)
        ]

    def scatter_copies(src, slot):
        out = []
        for k in range(1, nz):
            to = lax.rem(iz + k, nz)
            out.append(remote(
                src, rsbuf.at[slot, iz],
                rs_s.at[slot, k], rs_v.at[slot, k], {"group": to},
            ))
        return out

    def gathered_sum(src, slot, copies):
        rsbuf[slot, iz] = src[...]
        for c in copies:
            c.wait_recv()
        total = rsbuf[slot, 0]
        for k in range(1, nz):
            total = total + rsbuf[slot, k]
        return total

    dens_t = [dens[:, k * LANES:(k + 1) * LANES] for k in range(nt)]

    def first(g, carry):
        oe, oa, ow, em = carry
        a = [
            opac[g, :, k * LANES:(k + 1) * LANES].astype(jnp.float32) * dens_t[k]
            for k in range(nt)
        ]
        for k in range(nt):
            a_x[g, own, k * LANES:(k + 1) * LANES] = a[k]
            e_x[g, own, k * LANES:(k + 1) * LANES] = rad[g, :, k * LANES:(k + 1) * LANES]
        aw = [t * wts[g] for t in a]
        em = tuple(em[k] + aw[k] for k in range(nt))
        return pack(load(rad, g, slice(None)), g, oe), pack(a, g, oa), pack(aw, g, ow), em

    oe, oa, ow, em = lax.fori_loop(0, ng, first, (zero_pack, zero_pack, zero_pack, zero_tiles))
    o_aw[...] = ow
    o_ea[0] = oe
    o_ea[1] = oa
    put_tiles(emis, em)
    rows = sum(jnp.sum(t, axis=1, keepdims=True) for t in dens_t)
    rows_src[...] = jnp.broadcast_to(rows, (nrow, LANES))

    pl.semaphore_wait(barrier, plane - 1 + nz - 1)

    ea = (
        slab_copies(e_x, SUB, nrow, e_x, 0)
        + slab_copies(a_x, SUB, nrow, a_x, 1)
        + pol_copies(o_ea, hl_ea, hr_ea, 0)
    )
    start(ea)
    emit = scatter_copies(emis, ITERS)
    for c in emit:
        c.start()
    prefix = []
    for k in range(1, npol):
        to = lax.rem(ip + k, npol)
        prefix.append((
            ip + k < npol, ip - k >= 0,
            remote(rows_src, rows_buf.at[ip], row_s.at[k], row_v.at[k], {"polar": to}),
        ))
    for sends, _, c in prefix:
        @pl.when(sends)
        def _():
            c.start()

    tri = (
        lax.broadcasted_iota(jnp.int32, (ncol, ncol), 0)
        <= lax.broadcasted_iota(jnp.int32, (ncol, ncol), 1)
    ).astype(jnp.float32)
    within = jnp.dot(dens[...], tri, precision=HI, preferred_element_type=jnp.float32)
    col_out[...] = within
    finish(ea)

    x_e = both(hl_ea, hr_ea, 0)
    x_a = both(hl_ea, hr_ea, 1)
    halo_x[...] = x_e

    def second(g, od):
        v = load(e_x, g, slice(None))
        a = load(a_x, g, own)
        x = halo_x[own]
        v_own = [t[own] for t in v]
        lft, rgt = left_of(v_own, x, g), right_of(v_own, x, g)
        d = []
        for k in range(nt):
            rs = 0.5 * (below(v[k])[own] - above(v[k])[own])
            ps = 0.5 * (rgt[k] - lft[k])
            s = jnp.sqrt(rs * rs + ps * ps)
            q = a[k] * v_own[k]
            d.append(v_own[k] * (2.0 * q + s) / (6.0 * q * q + 3.0 * q * s + s * s))
            d_x[g, own, k * LANES:(k + 1) * LANES] = d[k]
        return pack(d, g, od)

    o_d[0] = lax.fori_loop(0, ng, second, zero_pack)
    dd = slab_copies(d_x, SUB, nrow, d_x, 2) + pol_copies(o_d, hl_d, hr_d, 1) + diag_copies(
        o_d, hl_d, hr_d, 0
    )
    start(dd)

    for _, comes, c in prefix:
        @pl.when(comes)
        def _():
            c.wait_recv()
    carried = rows_buf[0]
    for k in range(1, npol):
        carried = carried + rows_buf[k]
    diag = (
        lax.broadcasted_iota(jnp.int32, (nrow, nrow), 0)
        == lax.broadcasted_iota(jnp.int32, (nrow, nrow), 1)
    )
    flux_col = jnp.sum(jnp.where(diag, flux[...], 0.0), axis=1, keepdims=True)
    fix = []
    for k in range(nt):
        sl = slice(k * LANES, (k + 1) * LANES)
        column = (2.0 / (ncol * npol)) * (carried + col_out[:, sl])
        col_out[:, sl] = column
        fix.append(
            16.0 * dens_t[k] * mat0[:, sl] + flux_col * dens_t[k] * jnp.exp(-column)
        )
    put_tiles(fixed, fix)
    put_tiles(capac, [16.0 * t for t in dens_t])
    emission = gathered_sum(emis, ITERS, emit)
    mine = pl.ds(0, tiles)
    capac[mine] = capac[mine] + emission
    finish(dd)

    x_d = both(hl_d, hr_d, 0)
    d_in, d_out = inner_of(o_d[0]), outer_of(x_d)[own]
    x_mid = x_d[own]
    p_in, p_out = harm(x_mid, d_in), harm(x_mid, d_out)
    p_up, p_dn = harm(x_mid, above(x_d)[own]), harm(x_mid, below(x_d)[own])
    p_dg = 1.0 + x_a[own] + p_in + p_out + p_up + p_dn
    halo_ar[0] = p_in
    halo_ar[1] = p_out
    halo_ar[2] = p_up
    halo_ar[3] = p_dn
    halo_ar[4] = p_dg
    gsum[...] = jnp.zeros(gsum.shape, jnp.float32)
    hl_d[0] = x_d

    def third(g, o):
        d = load(d_x, g, slice(None))
        a = load(a_x, g, slice(None))
        v = load(e_x, g, slice(None))
        x = hl_d[0]
        xe = halo_x[own]
        dl, dr = left_of(d, x, g), right_of(d, x, g)
        v_own = [t[own] for t in v]
        vl, vr = left_of(v_own, xe, g), right_of(v_own, xe, g)
        res = []
        for k in range(nt):
            sl = slice(k * LANES, (k + 1) * LANES)
            fl, fr, fu = harm(d[k], dl[k]), harm(d[k], dr[k]), harm(d[k], above(d[k]))
            fd = below(fu)
            dg = 1.0 + a[k] + fl + fr + fu + fd
            fl_x[g, :, sl] = fl
            fr_x[g, :, sl] = fr
            fu_x[g, :, sl] = fu
            fd_x[g, :, sl] = fd
            dg_x[g, :, sl] = dg
            c = v_own[k]
            ao = a[k][own]
            image = (
                (1.0 + ao) * c
                + fu[own] * (c - above(v[k])[own])
                + fd[own] * (c - below(v[k])[own])
                + fl[own] * (c - vl[k])
                + fr[own] * (c - vr[k])
            )
            r = c - image
            res.append(r)
            r_x[g, own, sl] = r
            e_out[g, :, sl] = c
        return pack(res, g, o)

    o_r[0] = lax.fori_loop(0, ng, third, zero_pack)
    m_out[...] = mat0[...]
    dmat[...] = mat0[...]

    ones = jnp.ones((SUB, LANES), jnp.float32)
    quants = 4 * ng
    pick = (
        lax.broadcasted_iota(jnp.int32, (quants, LANES), 0)
        == lax.broadcasted_iota(jnp.int32, (quants, LANES), 1)
    )

    @pl.loop(0, ITERS)
    def _(it):
        lo, hi = dmat[:, :LANES], dmat[:, ncol - LANES:]
        even = lane_own % 2 == 0
        first_two = jnp.where(even, lo[:, 0:1], lo[:, 1:2])
        last_two = jnp.where(even, hi[:, LANES - 2:LANES - 1], hi[:, LANES - 1:LANES])
        o_r[0] = o_r[0] + o_aw[...] * jnp.where(lane_own < LANES // 2, first_two, last_two)
        sides = pol_copies(o_r, hl_r, hr_r, 2) + diag_copies(o_r, hl_r, hr_r, 1)
        slabs = slab_copies(r_x, SUB, nrow, r_x, 3)
        start(sides)

        @pl.loop(0, ng)
        def _(g):
            for base in (0, nrow - SUB):
                rows_x, rows_m = slice(SUB + base, 2 * SUB + base), slice(base, base + SUB)
                r_x[g, rows_x, :] = r_x[g, rows_x, :] + a_x[g, rows_x, :] * wts[g] * dmat[rows_m, :]

        start(slabs)
        mid = slice(2 * SUB, nrow)
        mid_m = slice(SUB, nrow - SUB)
        no_halo = jnp.zeros((nrow - 2 * SUB, LANES), jnp.float32)

        def stencil(g, rows, v, up, dn, vl, vr):
            out = []
            for k in range(nt):
                sl = slice(k * LANES, (k + 1) * LANES)
                out.append(
                    dg_x[g, rows, sl] * v[k]
                    - fu_x[g, rows, sl] * up[k]
                    - fd_x[g, rows, sl] * dn[k]
                    - fl_x[g, rows, sl] * vl[k]
                    - fr_x[g, rows, sl] * vr[k]
                )
            return out

        @pl.loop(0, ng)
        def _(g):
            v, full = [], []
            for k in range(nt):
                sl = slice(k * LANES, (k + 1) * LANES)
                r = r_x[g, mid, sl] + a_x[g, mid, sl] * wts[g] * dmat[mid_m, sl]
                r_x[g, mid, sl] = r
                v.append(r)
                full.append(jnp.concatenate(
                    [r_x[g, SUB:2 * SUB, sl], r, r_x[g, nrow:nrow + SUB, sl]], axis=0
                ))
            inner = slice(SUB, nrow - SUB)
            w = stencil(
                g, mid, v, [above(t)[inner] for t in full], [below(t)[inner] for t in full],
                left_of(v, no_halo, g), right_of(v, no_halo, g),
            )
            for k in range(nt):
                ar[g, mid_m, k * LANES:(k + 1) * LANES] = w[k]

        finish(sides + slabs)
        x_r = both(hl_r, hr_r, 0)
        halo_x[...] = x_r
        x_own = x_r[own]
        halo_ar[5] = (
            halo_ar[4] * x_own
            - halo_ar[0] * inner_of(o_r[0])
            - halo_ar[1] * outer_of(x_r)[own]
            - halo_ar[2] * above(x_r)[own]
            - halo_ar[3] * below(x_r)[own]
        )

        @pl.loop(0, ng)
        def _(g):
            x = halo_x[...]

            def end_rows(rows, window, keep):
                full = load(r_x, g, window)
                v = [t[keep] for t in full]
                return stencil(
                    g, rows, v, [above(t)[keep] for t in full], [below(t)[keep] for t in full],
                    left_of(v, x[rows], g), right_of(v, x[rows], g),
                )

            top = end_rows(slice(0, 2 * SUB), slice(0, 3 * SUB), slice(0, 2 * SUB))
            bot = end_rows(slice(nrow, next_), slice(nrow - SUB, next_), slice(SUB, 3 * SUB))
            w_mid = load(ar, g, mid_m)
            lane_mid = lane_of(nrow - 2 * SUB)
            hl = pltpu.roll(x[mid], LANES // 2 - 1 - 2 * g, 1)
            hr = pltpu.roll(x[mid], LANES - 1 - 2 * g, 1)
            w_mid[0] = w_mid[0] - jnp.where(lane_mid == 0, fl_x[g, mid, :LANES] * hl, 0.0)
            w_mid[-1] = w_mid[-1] - jnp.where(
                lane_mid == LANES - 1, fr_x[g, mid, ncol - LANES:] * hr, 0.0
            )
            w = [jnp.concatenate(parts, axis=0) for parts in zip(top, w_mid, bot)]
            v = load(r_x, g, own)
            w_own = [t[own] for t in w]
            wx = halo_ar[5]
            wl, wr = left_of(w_own, wx, g), right_of(w_own, wx, g)
            sums = [0.0, 0.0, 0.0, 0.0]
            for k in range(nt):
                sl = slice(k * LANES, (k + 1) * LANES)
                c = w_own[k]
                t = (
                    dg_x[g, own, sl] * c
                    - fu_x[g, own, sl] * above(w[k])[own]
                    - fd_x[g, own, sl] * below(w[k])[own]
                    - fl_x[g, own, sl] * wl[k]
                    - fr_x[g, own, sl] * wr[k]
                )
                ar[g, :, sl] = c
                aar[g, :, sl] = t
                r = v[k]
                for i, (p, q) in enumerate(((r, r), (r, c), (c, c), (c, t))):
                    sums[i] = sums[i] + jnp.sum(p * q, axis=0, keepdims=True)
            for i in range(4):
                gsum[pl.ds(i * ng + g, 1), :] = sums[i]

        gram[it, me] = lax.dot_general(
            ones, gsum[...], (((1,), (1,)), ((), ())), precision=HI,
            preferred_element_type=jnp.float32,
        )

        def gram_copy(k):
            _, where = plane_id(k)
            return remote(
                gram.at[it, me], gram.at[it, me], gram_s.at[k], gram_v.at[it, k], where
            )

        @pl.loop(1, plane)
        def _(k):
            gram_copy(k).start()

        @pl.loop(1, plane)
        def _(k):
            c = gram_copy(k)
            c.wait_recv()
            c.wait_send()

        total = lax.fori_loop(
            0, plane, lambda k, s: s + gram[it, k], jnp.zeros((SUB, LANES), jnp.float32)
        )
        spread = jnp.sum(jnp.where(pick, total[0:1], 0.0), axis=1, keepdims=True)
        norm_first = spread[0:ng]
        first_curv = spread[ng:2 * ng]
        image_norm = spread[2 * ng:3 * ng]
        image_twice = spread[3 * ng:4 * ng]
        step_first = norm_first / first_curv
        norm_second = (
            norm_first - 2.0 * step_first * first_curv + step_first * step_first * image_norm
        )
        scaled = 1.0 + norm_second / norm_first
        second_curv = (
            scaled * scaled * first_curv
            - scaled * step_first * (2.0 * image_norm)
            + step_first * step_first * image_twice
        )
        step_second = norm_second / second_curv
        cres[...] = jnp.broadcast_to(step_first + step_second * scaled, (ng, LANES))
        cimg[...] = jnp.broadcast_to(step_second * step_first, (ng, LANES))

        def update(g, absorbed):
            cr = cres[pl.ds(g, 1), :]
            ci = cimg[pl.ds(g, 1), :]
            out = []
            for k in range(nt):
                sl = slice(k * LANES, (k + 1) * LANES)
                r, w = r_x[g, own, sl], ar[g, :, sl]
                e = e_out[g, :, sl] + cr * r - ci * w
                e_out[g, :, sl] = e
                out.append(absorbed[k] + a_x[g, own, sl] * e)
            return tuple(out)

        put_tiles(absb, lax.fori_loop(0, ng, update, zero_tiles))
        send = scatter_copies(absb, it)
        for c in send:
            c.start()

        @pl.when(it + 1 < ITERS)
        def _():
            def trail(g, o):
                cr = cres[pl.ds(g, 1), :]
                ci = cimg[pl.ds(g, 1), :]
                res = []
                for k in range(nt):
                    sl = slice(k * LANES, (k + 1) * LANES)
                    r = r_x[g, own, sl] - cr * ar[g, :, sl] + ci * aar[g, :, sl]
                    r_x[g, own, sl] = r
                    res.append(r)
                return pack(res, g, o)

            o_r[0] = lax.fori_loop(0, ng, trail, zero_pack)

        mnext[it, mine] = (fixed[mine] + gathered_sum(absb, it, send)) / capac[mine]
        for c in send:
            c.wait_send()
        news = get_tiles(mnext.at[it])
        for k in range(nt):
            sl = slice(k * LANES, (k + 1) * LANES)
            dmat[:, sl] = news[k] - m_out[:, sl]
            m_out[:, sl] = news[k]

    for c in emit:
        c.wait_send()
    for sends, _, c in prefix:
        @pl.when(sends)
        def _():
            c.wait_send()


def per_device(nr, npol, nz, density, opacity, radiation_old, material_old, weights, stellar_flux):
    ng, nrow, ncol = radiation_old.shape
    f32 = jnp.float32
    ext, inner = (ng, nrow + 2 * SUB, ncol), (ng, nrow, ncol)
    tiles = (nrow // SUB) * (ncol // LANES)
    plane = nr * npol
    vm = lambda *shape: pltpu.VMEM(shape, f32)
    packed, around = (nrow, LANES), (nrow + 2 * SUB, LANES)
    dma = lambda *shape: pltpu.SemaphoreType.DMA(shape)
    scratch = (
        [vm(*ext) for _ in range(9)]
        + [vm(*inner), vm(*inner)]
        + [vm(2, *packed), vm(2, *around), vm(2, *around)]
        + [vm(1, *packed), vm(1, *around), vm(1, *around)] * 2
        + [vm(*packed), vm(*around), vm(6, *packed), vm(LANES, LANES), vm(ITERS, plane, SUB, LANES)]
        + [vm(ng, LANES), vm(ng, LANES)]
        + [vm(*packed), vm(npol, *packed), vm(tiles, SUB, LANES), vm(tiles, SUB, LANES)]
        + [vm(ITERS + 1, nz, tiles, SUB, LANES), vm(ITERS, tiles, SUB, LANES)]
        + [vm(tiles, SUB, LANES), vm(tiles, SUB, LANES), vm(nrow, ncol)]
        + [dma(4, 2), dma(4, 2), dma(3, 2), dma(3, 2), dma(2, 4), dma(2, 4)]
        + [dma(plane), dma(ITERS, plane), dma(ITERS + 1, nz), dma(ITERS + 1, nz)]
        + [dma(ITERS, nz), dma(ITERS, nz), dma(npol), dma(npol)]
    )
    in_vmem = pl.BlockSpec(memory_space=pltpu.VMEM)
    return pl.pallas_call(
        functools.partial(kernel, nr, npol, nz),
        out_shape=[
            jax.ShapeDtypeStruct(inner, f32),
            jax.ShapeDtypeStruct((nrow, ncol), f32),
            jax.ShapeDtypeStruct((nrow, ncol), f32),
        ],
        in_specs=[in_vmem] * 4 + [pl.BlockSpec(memory_space=pltpu.SMEM), in_vmem],
        out_specs=[in_vmem] * 3,
        scratch_shapes=scratch,
        compiler_params=pltpu.CompilerParams(
            collective_id=0, has_side_effects=True, vmem_limit_bytes=48 * 1024 * 1024
        ),
    )(density, opacity, radiation_old, material_old, weights, stellar_flux.reshape(1, -1))


def solution(mesh):
    sizes = (mesh.shape["radius"], mesh.shape["polar"], mesh.shape["group"])
    return jax.shard_map(
        functools.partial(per_device, *sizes),
        mesh=mesh,
        in_specs=(
            P("radius", "polar"),
            P("group", "radius", "polar"),
            P("group", "radius", "polar"),
            P("radius", "polar"),
            P("group"),
            P("radius"),
        ),
        out_specs=(P("group", "radius", "polar"), P("radius", "polar"), P("radius", "polar")),
        check_vma=False,
    )
```

```python
import functools

import jax
import jax.numpy as jnp
from jax import lax
from jax.experimental import pallas as pl
from jax.experimental.pallas import tpu as pltpu
from jax.sharding import PartitionSpec as P

ITERS = 3
LANES = 128
SUB = 8
MESH = pl.DeviceIdType.MESH
HI = lax.Precision.HIGHEST


def harm(a, b):
    total = a + b
    return 2.0 * a * b / jnp.where(total > 0.0, total, 1.0)


def kernel(
    nr, npol, nz,
    dens, opac, rad, mat0, wts, flux,
    e_out, m_out, col_out,
    e_x, a_x, d_x, r_x, dg_x, fu_x, fd_x, fl_x, fr_x, ar, aar,
    o_ea, hl_ea, hr_ea, o_d, hl_d, hr_d, o_r, hl_r, hr_r,
    o_aw, halo_x, halo_ar, gsum, gram, cres, cimg,
    rows_src, rows_buf, absb, emis, rsbuf, mnext, fixed, capac, dmat,
    slab_s, slab_v, pol_s, pol_v, diag_s, diag_v,
    gram_s, gram_v, rs_s, rs_v, ag_s, ag_v, row_s, row_v,
):
    ng, nrow, ncol = rad.shape
    nt = ncol // LANES
    next_ = nrow + 2 * SUB
    own = slice(SUB, SUB + nrow)
    tiles = (nrow // SUB) * nt
    tp = tiles // nz
    plane = nr * npol

    ir = lax.axis_index("radius")
    ip = lax.axis_index("polar")
    iz = lax.axis_index("group")
    me = ir * npol + ip

    def lane_of(n):
        return lax.broadcasted_iota(jnp.int32, (n, LANES), 1)

    lane_own, lane_ext = lane_of(nrow), lane_of(next_)

    def zeros_at(ref, *idx):
        ref[idx] = jnp.zeros(ref.at[idx].shape, ref.dtype)

    for ref in (e_x, a_x, d_x, r_x):
        zeros_at(ref, slice(None), slice(0, SUB), slice(None))
        zeros_at(ref, slice(None), slice(SUB + nrow, next_), slice(None))
    for ref in (hl_ea, hr_ea, hl_d, hr_d, hl_r, hr_r, rows_buf):
        ref[...] = jnp.zeros(ref.shape, ref.dtype)

    barrier = pltpu.get_barrier_semaphore()

    def plane_id(k):
        other = lax.rem(me + k, plane)
        return other, {"radius": other // npol, "polar": lax.rem(other, npol)}

    @pl.loop(1, plane)
    def _(k):
        _, where = plane_id(k)
        pl.semaphore_signal(barrier, inc=1, device_id=where, device_id_type=MESH)

    for k in range(1, nz):
        pl.semaphore_signal(
            barrier, inc=1, device_id={"group": lax.rem(iz + k, nz)}, device_id_type=MESH
        )

    def remote(src, dst, ssem, rsem, where):
        return pltpu.make_async_remote_copy(
            src_ref=src, dst_ref=dst, send_sem=ssem, recv_sem=rsem,
            device_id=where, device_id_type=MESH,
        )

    def near(dr, dp):
        return {"radius": lax.rem(ir + dr + nr, nr), "polar": lax.rem(ip + dp + npol, npol)}

    def inside(dr, dp):
        r, p = ir + dr, ip + dp
        return (r >= 0) & (r < nr) & (p >= 0) & (p < npol)

    def slab_copies(src_ref, lo, hi, dst_ref, f):
        out = []
        for i, dr in enumerate((-1, 1)):
            src = src_ref.at[:, pl.ds(lo if dr < 0 else hi, SUB), :]
            dst = dst_ref.at[:, pl.ds(SUB + nrow if dr < 0 else 0, SUB), :]
            out.append((dr, 0, remote(src, dst, slab_s.at[f, i], slab_v.at[f, i], near(dr, 0))))
        return out

    def pol_copies(o, hl, hr, f):
        out = []
        for i, dp in enumerate((-1, 1)):
            dst = (hr if dp < 0 else hl).at[:, pl.ds(SUB, nrow), :]
            out.append((0, dp, remote(o, dst, pol_s.at[f, i], pol_v.at[f, i], near(0, dp))))
        return out

    def diag_copies(o, hl, hr, f):
        out = []
        for i, (dr, dp) in enumerate(((-1, -1), (-1, 1), (1, -1), (1, 1))):
            src = o.at[:, pl.ds(0 if dr < 0 else nrow - SUB, SUB), :]
            dst = (hr if dp < 0 else hl).at[:, pl.ds(SUB + nrow if dr < 0 else 0, SUB), :]
            out.append((dr, dp, remote(src, dst, diag_s.at[f, i], diag_v.at[f, i], near(dr, dp))))
        return out

    def start(copies):
        for dr, dp, c in copies:
            @pl.when(inside(dr, dp))
            def _():
                c.start()

    def finish(copies):
        for dr, dp, c in copies:
            @pl.when(inside(-dr, -dp))
            def _():
                c.wait_recv()
        for dr, dp, c in copies:
            @pl.when(inside(dr, dp))
            def _():
                c.wait_send()

    def load(ref, g, rows):
        return [ref[g, rows, k * LANES:(k + 1) * LANES] for k in range(nt)]

    def pack(tiles_in, g, into):
        left = pltpu.roll(tiles_in[0], 2 * g, 1)
        right = pltpu.roll(tiles_in[-1], lax.rem(2 * g + LANES // 2 + 2, LANES), 1)
        half = lane_own // 2
        into = jnp.where(half == g, left, into)
        return jnp.where(half == g + LANES // 4, right, into)

    def left_of(v, halo, g):
        n = v[0].shape[0]
        edge = lane_of(n) == 0
        turned = [pltpu.roll(t, 1, 1) for t in v]
        before = [pltpu.roll(halo, LANES // 2 - 1 - 2 * g, 1)] + turned[:-1]
        return [jnp.where(edge, b, t) for b, t in zip(before, turned)]

    def right_of(v, halo, g):
        n = v[0].shape[0]
        edge = lane_of(n) == LANES - 1
        turned = [pltpu.roll(t, LANES - 1, 1) for t in v]
        after = turned[1:] + [pltpu.roll(halo, LANES - 1 - 2 * g, 1)]
        return [jnp.where(edge, b, t) for b, t in zip(after, turned)]

    def above(t):
        return pltpu.roll(t, 1, 0)

    def below(t):
        return pltpu.roll(t, t.shape[0] - 1, 0)

    def both(hl, hr, k):
        return jnp.where(lane_ext < LANES // 2, hr[k], hl[k])

    def outer_of(x):
        n = x.shape[0]
        return jnp.where(lane_of(n) < LANES // 2, pltpu.roll(x, LANES - 1, 1), pltpu.roll(x, 1, 1))

    def inner_of(o):
        return jnp.where(
            lane_own < LANES // 2,
            pltpu.roll(o, LANES // 2 - 1, 1),
            pltpu.roll(o, LANES // 2 + 1, 1),
        )

    zero_pack = jnp.zeros((nrow, LANES), jnp.float32)
    zero_tiles = tuple(jnp.zeros((nrow, LANES), jnp.float32) for _ in range(nt))

    def put_tiles(ref, parts):
        for k, part in enumerate(parts):
            for i in range(nrow // SUB):
                ref[k * (nrow // SUB) + i] = part[i * SUB:(i + 1) * SUB]

    def get_tiles(ref):
        per = nrow // SUB
        return [
            jnp.concatenate([ref[k * per + i] for i in range(per)], axis=0) for k in range(nt)
        ]

    def scatter_copies(src, slot):
        out = []
        for k in range(1, nz):
            to = lax.rem(iz + k, nz)
            out.append(remote(
                src, rsbuf.at[slot, iz],
                rs_s.at[slot, k], rs_v.at[slot, k], {"group": to},
            ))
        return out

    def gathered_sum(src, slot, copies):
        rsbuf[slot, iz] = src[...]
        for c in copies:
            c.wait_recv()
        total = rsbuf[slot, 0]
        for k in range(1, nz):
            total = total + rsbuf[slot, k]
        return total

    dens_t = [dens[:, k * LANES:(k + 1) * LANES] for k in range(nt)]

    def first(g, carry):
        oe, oa, ow, em = carry
        a = [
            opac[g, :, k * LANES:(k + 1) * LANES].astype(jnp.float32) * dens_t[k]
            for k in range(nt)
        ]
        for k in range(nt):
            a_x[g, own, k * LANES:(k + 1) * LANES] = a[k]
            e_x[g, own, k * LANES:(k + 1) * LANES] = rad[g, :, k * LANES:(k + 1) * LANES]
        aw = [t * wts[g] for t in a]
        em = tuple(em[k] + aw[k] for k in range(nt))
        return pack(load(rad, g, slice(None)), g, oe), pack(a, g, oa), pack(aw, g, ow), em

    oe, oa, ow, em = lax.fori_loop(0, ng, first, (zero_pack, zero_pack, zero_pack, zero_tiles), unroll=2)
    o_aw[...] = ow
    o_ea[0] = oe
    o_ea[1] = oa
    put_tiles(emis, em)
    rows = sum(jnp.sum(t, axis=1, keepdims=True) for t in dens_t)
    rows_src[...] = jnp.broadcast_to(rows, (nrow, LANES))

    pl.semaphore_wait(barrier, plane - 1 + nz - 1)

    ea = (
        slab_copies(e_x, SUB, nrow, e_x, 0)
        + slab_copies(a_x, SUB, nrow, a_x, 1)
        + pol_copies(o_ea, hl_ea, hr_ea, 0)
    )
    start(ea)
    emit = scatter_copies(emis, ITERS)
    for c in emit:
        c.start()
    prefix = []
    for k in range(1, npol):
        to = lax.rem(ip + k, npol)
        prefix.append((
            ip + k < npol, ip - k >= 0,
            remote(rows_src, rows_buf.at[ip], row_s.at[k], row_v.at[k], {"polar": to}),
        ))
    for sends, _, c in prefix:
        @pl.when(sends)
        def _():
            c.start()

    tri = (
        lax.broadcasted_iota(jnp.int32, (ncol, ncol), 0)
        <= lax.broadcasted_iota(jnp.int32, (ncol, ncol), 1)
    ).astype(jnp.float32)
    within = jnp.dot(dens[...], tri, precision=HI, preferred_element_type=jnp.float32)
    col_out[...] = within
    finish(ea)

    x_e = both(hl_ea, hr_ea, 0)
    x_a = both(hl_ea, hr_ea, 1)
    halo_x[...] = x_e

    def second(g, od):
        v = load(e_x, g, slice(None))
        a = load(a_x, g, own)
        x = halo_x[own]
        v_own = [t[own] for t in v]
        lft, rgt = left_of(v_own, x, g), right_of(v_own, x, g)
        d = []
        for k in range(nt):
            rs = 0.5 * (below(v[k])[own] - above(v[k])[own])
            ps = 0.5 * (rgt[k] - lft[k])
            s = jnp.sqrt(rs * rs + ps * ps)
            q = a[k] * v_own[k]
            d.append(v_own[k] * (2.0 * q + s) / (6.0 * q * q + 3.0 * q * s + s * s))
            d_x[g, own, k * LANES:(k + 1) * LANES] = d[k]
        return pack(d, g, od)

    o_d[0] = lax.fori_loop(0, ng, second, zero_pack, unroll=2)
    dd = slab_copies(d_x, SUB, nrow, d_x, 2) + pol_copies(o_d, hl_d, hr_d, 1) + diag_copies(
        o_d, hl_d, hr_d, 0
    )
    start(dd)

    for _, comes, c in prefix:
        @pl.when(comes)
        def _():
            c.wait_recv()
    carried = rows_buf[0]
    for k in range(1, npol):
        carried = carried + rows_buf[k]
    diag = (
        lax.broadcasted_iota(jnp.int32, (nrow, nrow), 0)
        == lax.broadcasted_iota(jnp.int32, (nrow, nrow), 1)
    )
    flux_col = jnp.sum(jnp.where(diag, flux[...], 0.0), axis=1, keepdims=True)
    fix = []
    for k in range(nt):
        sl = slice(k * LANES, (k + 1) * LANES)
        column = (2.0 / (ncol * npol)) * (carried + col_out[:, sl])
        col_out[:, sl] = column
        fix.append(
            16.0 * dens_t[k] * mat0[:, sl] + flux_col * dens_t[k] * jnp.exp(-column)
        )
    put_tiles(fixed, fix)
    put_tiles(capac, [16.0 * t for t in dens_t])
    emission = gathered_sum(emis, ITERS, emit)
    mine = pl.ds(0, tiles)
    capac[mine] = capac[mine] + emission
    finish(dd)

    x_d = both(hl_d, hr_d, 0)
    d_in, d_out = inner_of(o_d[0]), outer_of(x_d)[own]
    x_mid = x_d[own]
    p_in, p_out = harm(x_mid, d_in), harm(x_mid, d_out)
    p_up, p_dn = harm(x_mid, above(x_d)[own]), harm(x_mid, below(x_d)[own])
    p_dg = 1.0 + x_a[own] + p_in + p_out + p_up + p_dn
    halo_ar[0] = p_in
    halo_ar[1] = p_out
    halo_ar[2] = p_up
    halo_ar[3] = p_dn
    halo_ar[4] = p_dg
    gsum[...] = jnp.zeros(gsum.shape, jnp.float32)
    hl_d[0] = x_d

    def third(g, o):
        d = load(d_x, g, slice(None))
        a = load(a_x, g, slice(None))
        v = load(e_x, g, slice(None))
        x = hl_d[0]
        xe = halo_x[own]
        dl, dr = left_of(d, x, g), right_of(d, x, g)
        v_own = [t[own] for t in v]
        vl, vr = left_of(v_own, xe, g), right_of(v_own, xe, g)
        res = []
        for k in range(nt):
            sl = slice(k * LANES, (k + 1) * LANES)
            fl, fr, fu = harm(d[k], dl[k]), harm(d[k], dr[k]), harm(d[k], above(d[k]))
            fd = below(fu)
            dg = 1.0 + a[k] + fl + fr + fu + fd
            fl_x[g, :, sl] = fl
            fr_x[g, :, sl] = fr
            fu_x[g, :, sl] = fu
            fd_x[g, :, sl] = fd
            dg_x[g, :, sl] = dg
            c = v_own[k]
            ao = a[k][own]
            image = (
                (1.0 + ao) * c
                + fu[own] * (c - above(v[k])[own])
                + fd[own] * (c - below(v[k])[own])
                + fl[own] * (c - vl[k])
                + fr[own] * (c - vr[k])
            )
            r = c - image
            res.append(r)
            r_x[g, own, sl] = r
            e_out[g, :, sl] = c
        return pack(res, g, o)

    o_r[0] = lax.fori_loop(0, ng, third, zero_pack, unroll=2)
    m_out[...] = mat0[...]
    dmat[...] = mat0[...]

    ones = jnp.ones((SUB, LANES), jnp.float32)
    quants = 4 * ng
    pick = (
        lax.broadcasted_iota(jnp.int32, (quants, LANES), 0)
        == lax.broadcasted_iota(jnp.int32, (quants, LANES), 1)
    )

    @pl.loop(0, ITERS)
    def _(it):
        lo, hi = dmat[:, :LANES], dmat[:, ncol - LANES:]
        even = lane_own % 2 == 0
        first_two = jnp.where(even, lo[:, 0:1], lo[:, 1:2])
        last_two = jnp.where(even, hi[:, LANES - 2:LANES - 1], hi[:, LANES - 1:LANES])
        o_r[0] = o_r[0] + o_aw[...] * jnp.where(lane_own < LANES // 2, first_two, last_two)
        sides = pol_copies(o_r, hl_r, hr_r, 2) + diag_copies(o_r, hl_r, hr_r, 1)
        slabs = slab_copies(r_x, SUB, nrow, r_x, 3)
        start(sides)

        @pl.loop(0, ng, unroll=2)
        def _(g):
            for base in (0, nrow - SUB):
                rows_x, rows_m = slice(SUB + base, 2 * SUB + base), slice(base, base + SUB)
                r_x[g, rows_x, :] = r_x[g, rows_x, :] + a_x[g, rows_x, :] * wts[g] * dmat[rows_m, :]

        start(slabs)
        mid = slice(2 * SUB, nrow)
        mid_m = slice(SUB, nrow - SUB)
        no_halo = jnp.zeros((nrow - 2 * SUB, LANES), jnp.float32)

        def stencil(g, rows, v, up, dn, vl, vr):
            out = []
            for k in range(nt):
                sl = slice(k * LANES, (k + 1) * LANES)
                out.append(
                    dg_x[g, rows, sl] * v[k]
                    - fu_x[g, rows, sl] * up[k]
                    - fd_x[g, rows, sl] * dn[k]
                    - fl_x[g, rows, sl] * vl[k]
                    - fr_x[g, rows, sl] * vr[k]
                )
            return out

        @pl.loop(0, ng, unroll=2)
        def _(g):
            v, full = [], []
            for k in range(nt):
                sl = slice(k * LANES, (k + 1) * LANES)
                r = r_x[g, mid, sl] + a_x[g, mid, sl] * wts[g] * dmat[mid_m, sl]
                r_x[g, mid, sl] = r
                v.append(r)
                full.append(jnp.concatenate(
                    [r_x[g, SUB:2 * SUB, sl], r, r_x[g, nrow:nrow + SUB, sl]], axis=0
                ))
            inner = slice(SUB, nrow - SUB)
            w = stencil(
                g, mid, v, [above(t)[inner] for t in full], [below(t)[inner] for t in full],
                left_of(v, no_halo, g), right_of(v, no_halo, g),
            )
            for k in range(nt):
                ar[g, mid_m, k * LANES:(k + 1) * LANES] = w[k]

        finish(sides + slabs)
        x_r = both(hl_r, hr_r, 0)
        halo_x[...] = x_r
        x_own = x_r[own]
        halo_ar[5] = (
            halo_ar[4] * x_own
            - halo_ar[0] * inner_of(o_r[0])
            - halo_ar[1] * outer_of(x_r)[own]
            - halo_ar[2] * above(x_r)[own]
            - halo_ar[3] * below(x_r)[own]
        )

        @pl.loop(0, ng, unroll=2)
        def _(g):
            x = halo_x[...]

            def end_rows(rows, window, keep):
                full = load(r_x, g, window)
                v = [t[keep] for t in full]
                return stencil(
                    g, rows, v, [above(t)[keep] for t in full], [below(t)[keep] for t in full],
                    left_of(v, x[rows], g), right_of(v, x[rows], g),
                )

            top = end_rows(slice(0, 2 * SUB), slice(0, 3 * SUB), slice(0, 2 * SUB))
            bot = end_rows(slice(nrow, next_), slice(nrow - SUB, next_), slice(SUB, 3 * SUB))
            w_mid = load(ar, g, mid_m)
            lane_mid = lane_of(nrow - 2 * SUB)
            hl = pltpu.roll(x[mid], LANES // 2 - 1 - 2 * g, 1)
            hr = pltpu.roll(x[mid], LANES - 1 - 2 * g, 1)
            w_mid[0] = w_mid[0] - jnp.where(lane_mid == 0, fl_x[g, mid, :LANES] * hl, 0.0)
            w_mid[-1] = w_mid[-1] - jnp.where(
                lane_mid == LANES - 1, fr_x[g, mid, ncol - LANES:] * hr, 0.0
            )
            w = [jnp.concatenate(parts, axis=0) for parts in zip(top, w_mid, bot)]
            v = load(r_x, g, own)
            w_own = [t[own] for t in w]
            wx = halo_ar[5]
            wl, wr = left_of(w_own, wx, g), right_of(w_own, wx, g)
            sums = [0.0, 0.0, 0.0, 0.0]
            for k in range(nt):
                sl = slice(k * LANES, (k + 1) * LANES)
                c = w_own[k]
                t = (
                    dg_x[g, own, sl] * c
                    - fu_x[g, own, sl] * above(w[k])[own]
                    - fd_x[g, own, sl] * below(w[k])[own]
                    - fl_x[g, own, sl] * wl[k]
                    - fr_x[g, own, sl] * wr[k]
                )
                ar[g, :, sl] = c
                aar[g, :, sl] = t
                r = v[k]
                for i, (p, q) in enumerate(((r, r), (r, c), (c, c), (c, t))):
                    sums[i] = sums[i] + jnp.sum(p * q, axis=0, keepdims=True)
            for i in range(4):
                gsum[pl.ds(i * ng + g, 1), :] = sums[i]

        gram[it, me] = lax.dot_general(
            ones, gsum[...], (((1,), (1,)), ((), ())), precision=HI,
            preferred_element_type=jnp.float32,
        )

        def gram_copy(k):
            _, where = plane_id(k)
            return remote(
                gram.at[it, me], gram.at[it, me], gram_s.at[k], gram_v.at[it, k], where
            )

        @pl.loop(1, plane, unroll=min(plane - 1, 7))
        def _(k):
            gram_copy(k).start()

        @pl.loop(1, plane, unroll=min(plane - 1, 7))
        def _(k):
            c = gram_copy(k)
            c.wait_recv()
            c.wait_send()

        total = lax.fori_loop(
            0, plane, lambda k, s: s + gram[it, k], jnp.zeros((SUB, LANES), jnp.float32),
            unroll=min(plane, 8),
        )
        spread = jnp.sum(jnp.where(pick, total[0:1], 0.0), axis=1, keepdims=True)
        norm_first = spread[0:ng]
        first_curv = spread[ng:2 * ng]
        image_norm = spread[2 * ng:3 * ng]
        image_twice = spread[3 * ng:4 * ng]
        step_first = norm_first / first_curv
        norm_second = (
            norm_first - 2.0 * step_first * first_curv + step_first * step_first * image_norm
        )
        scaled = 1.0 + norm_second / norm_first
        second_curv = (
            scaled * scaled * first_curv
            - scaled * step_first * (2.0 * image_norm)
            + step_first * step_first * image_twice
        )
        step_second = norm_second / second_curv
        cres[...] = jnp.broadcast_to(step_first + step_second * scaled, (ng, LANES))
        cimg[...] = jnp.broadcast_to(step_second * step_first, (ng, LANES))

        def update(g, absorbed):
            cr = cres[pl.ds(g, 1), :]
            ci = cimg[pl.ds(g, 1), :]
            out = []
            for k in range(nt):
                sl = slice(k * LANES, (k + 1) * LANES)
                r, w = r_x[g, own, sl], ar[g, :, sl]
                e = e_out[g, :, sl] + cr * r - ci * w
                e_out[g, :, sl] = e
                out.append(absorbed[k] + a_x[g, own, sl] * e)
            return tuple(out)

        put_tiles(absb, lax.fori_loop(0, ng, update, zero_tiles, unroll=2))
        send = scatter_copies(absb, it)
        for c in send:
            c.start()

        @pl.when(it + 1 < ITERS)
        def _():
            def trail(g, o):
                cr = cres[pl.ds(g, 1), :]
                ci = cimg[pl.ds(g, 1), :]
                res = []
                for k in range(nt):
                    sl = slice(k * LANES, (k + 1) * LANES)
                    r = r_x[g, own, sl] - cr * ar[g, :, sl] + ci * aar[g, :, sl]
                    r_x[g, own, sl] = r
                    res.append(r)
                return pack(res, g, o)

            o_r[0] = lax.fori_loop(0, ng, trail, zero_pack, unroll=2)

        mnext[it, mine] = (fixed[mine] + gathered_sum(absb, it, send)) / capac[mine]
        for c in send:
            c.wait_send()
        news = get_tiles(mnext.at[it])
        for k in range(nt):
            sl = slice(k * LANES, (k + 1) * LANES)
            dmat[:, sl] = news[k] - m_out[:, sl]
            m_out[:, sl] = news[k]

    for c in emit:
        c.wait_send()
    for sends, _, c in prefix:
        @pl.when(sends)
        def _():
            c.wait_send()


def per_device(nr, npol, nz, density, opacity, radiation_old, material_old, weights, stellar_flux):
    ng, nrow, ncol = radiation_old.shape
    f32 = jnp.float32
    ext, inner = (ng, nrow + 2 * SUB, ncol), (ng, nrow, ncol)
    tiles = (nrow // SUB) * (ncol // LANES)
    plane = nr * npol
    vm = lambda *shape: pltpu.VMEM(shape, f32)
    packed, around = (nrow, LANES), (nrow + 2 * SUB, LANES)
    dma = lambda *shape: pltpu.SemaphoreType.DMA(shape)
    scratch = (
        [vm(*ext) for _ in range(9)]
        + [vm(*inner), vm(*inner)]
        + [vm(2, *packed), vm(2, *around), vm(2, *around)]
        + [vm(1, *packed), vm(1, *around), vm(1, *around)] * 2
        + [vm(*packed), vm(*around), vm(6, *packed), vm(LANES, LANES), vm(ITERS, plane, SUB, LANES)]
        + [vm(ng, LANES), vm(ng, LANES)]
        + [vm(*packed), vm(npol, *packed), vm(tiles, SUB, LANES), vm(tiles, SUB, LANES)]
        + [vm(ITERS + 1, nz, tiles, SUB, LANES), vm(ITERS, tiles, SUB, LANES)]
        + [vm(tiles, SUB, LANES), vm(tiles, SUB, LANES), vm(nrow, ncol)]
        + [dma(4, 2), dma(4, 2), dma(3, 2), dma(3, 2), dma(2, 4), dma(2, 4)]
        + [dma(plane), dma(ITERS, plane), dma(ITERS + 1, nz), dma(ITERS + 1, nz)]
        + [dma(ITERS, nz), dma(ITERS, nz), dma(npol), dma(npol)]
    )
    in_vmem = pl.BlockSpec(memory_space=pltpu.VMEM)
    return pl.pallas_call(
        functools.partial(kernel, nr, npol, nz),
        out_shape=[
            jax.ShapeDtypeStruct(inner, f32),
            jax.ShapeDtypeStruct((nrow, ncol), f32),
            jax.ShapeDtypeStruct((nrow, ncol), f32),
        ],
        in_specs=[in_vmem] * 4 + [pl.BlockSpec(memory_space=pltpu.SMEM), in_vmem],
        out_specs=[in_vmem] * 3,
        scratch_shapes=scratch,
        compiler_params=pltpu.CompilerParams(
            collective_id=0, has_side_effects=True, vmem_limit_bytes=48 * 1024 * 1024
        ),
    )(density, opacity, radiation_old, material_old, weights, stellar_flux.reshape(1, -1))


def solution(mesh):
    sizes = (mesh.shape["radius"], mesh.shape["polar"], mesh.shape["group"])
    return jax.shard_map(
        functools.partial(per_device, *sizes),
        mesh=mesh,
        in_specs=(
            P("radius", "polar"),
            P("group", "radius", "polar"),
            P("group", "radius", "polar"),
            P("radius", "polar"),
            P("group"),
            P("radius"),
        ),
        out_specs=(P("group", "radius", "polar"), P("radius", "polar"), P("radius", "polar")),
        check_vma=False,
    )
```
